32 devices in a mesh: job: 2 (over y), cuts: 4 (over x, core), mesh: 4 (over z).
Axes of the slice: x: 2, y: 2, z: 4, core: 2. Of those that a mesh axis runs over, the one named last changes fastest.
Arguments:
- blocks: bfloat16 [512, 12288], P(('job', 'cuts'), 'mesh'), parts along dimension 0, may hold values from -6 to 6
- boundary_shift: int32 [8], P(('job', 'cuts')), parts along dimension 0, may hold values from -32 to 32, as said below
- centre: float32 [8], P(('job', 'cuts')), parts along dimension 0, may hold values from -1 to 1
- half_width: float32 [8], P(('job', 'cuts')), parts along dimension 0, may hold values from 1 to 2
- cell_matrix: bfloat16 [216, 216], replicated, may hold values from -0.4375 to 0.4375
- cell_coef: float32 [256], P(('job', 'mesh')), parts along dimension 0, may hold values from 0.3 to 1.5
- connectivity: int32 [216, 256], P(None, ('job', 'mesh')), parts along dimension 1, may hold values from 0 to 3327
- halo_list: int32 [2048], P(('job', 'mesh')), parts along dimension 0, may hold values from 0 to 3071, as said below
- mass: float32 [24576], P(('job', 'mesh')), parts along dimension 0, may hold values from 0.5 to 3.6
- potential: float32 [24576], P(('job', 'mesh')), parts along dimension 0, may hold values from 0.2 to 1
Outputs:
- filtered: float32 [512, 12288], P(('job', 'cuts'), 'mesh'), parts along dimension 0
The draws below stay inside these ranges and needn't reach their ends.
There are 2 independent parts, one for each index of `job`. The reference program is written for one: setup_inputs(seed, part) draws one part's arguments, and reference() takes and returns one part's arrays. A program takes and returns all parts, laid end to end along the dimension named above; an argument that names none is the same for every part. Nothing has to cross between parts.
Inputs may be any that keep to these rules, and one draw needn't show every extreme that they name: `boundary_shift`: every entry lies within 32 in size; the first slice's is not negative and the last slice's not positive; both ends of the range are reached. `halo_list`: the 256 entries of each device's list are distinct owned nodes, and each list holds 0 and 3071.
All inputs are finite; a program needn't handle non-finite values.
Results may differ from the reference program's by a relative error of at most 0.0028.
Values may be sent and summed in bfloat16 or wider, within the bound.
A program may use at most 64 MiB of HBM per device.

```python
import math
import jax
import jax.numpy as jnp
from jax import lax

BLOCK = 64
CELL_NODES = 216
NODES_DEV = 3072
CELLS_DEV = 32
GHOST = 256
TOTAL = 12288
CELLS = 128
STATES = 256
N_CUTS = 4
N_MESH = 4


def draw_boundary_shift(key, part):
    key = jax.random.fold_in(key, 11)
    first_key, second_key = jax.random.split(key)
    half_rows = BLOCK // 2
    shifts = jax.random.randint(first_key, (N_CUTS,), -half_rows, half_rows + 1)
    shifts = shifts.at[0].set(jnp.abs(shifts[0]))
    shifts = shifts.at[N_CUTS - 1].set(-jnp.abs(shifts[N_CUTS - 1]))
    picked = jax.random.permutation(second_key, N_CUTS - 2) + 1
    shifts = shifts.at[picked[0]].set(half_rows)
    shifts = shifts.at[picked[1]].set(-half_rows)
    return shifts.astype(jnp.int32)


def draw_halo_list(key, part):
    key = jax.random.fold_in(key, 23)

    def one_list(device_key):
        first_key, second_key = jax.random.split(device_key)
        inner = jax.random.permutation(first_key, NODES_DEV - 2)[:GHOST - 2] + 1
        ends = jnp.array([0, NODES_DEV - 1], dtype=jnp.int32)
        chosen = jnp.concatenate([ends, inner.astype(jnp.int32)])
        return jax.random.permutation(second_key, chosen)
    lists = jax.vmap(one_list)(jax.random.split(key, N_MESH))
    return lists.reshape(-1).astype(jnp.int32)


def draw_mass(key, part):
    key = jax.random.fold_in(key, 37)
    count = NODES_DEV * N_MESH
    ramp = 1.0 + 2.0 * jnp.arange(count, dtype=jnp.float32) / (count - 1)
    spread = jnp.exp(jax.random.uniform(key, (count,), jnp.float32, math.log(0.5), math.log(1.2)))
    return (spread * ramp).astype(jnp.float32)


def place_ends(drawn, own_key, least, high):
    shape = drawn.shape
    spot = [jax.random.randint(jax.random.fold_in(own_key, axis), (), 0, shape[axis]) for axis in range(len(shape))]
    drawn = drawn.at[tuple(spot)].set(least)
    longest = shape.index(max(shape))
    spot[longest] = (spot[longest] + 1) % shape[longest]
    return drawn.at[tuple(spot)].set(high)


def steps_of(stream_key, shape, cuts, least, largest):
    gain, own = 1.0, jax.random.fold_in(stream_key, 6)
    for axis_at, parts in cuts:
        heights = jnp.exp(jax.random.uniform(jax.random.fold_in(own, axis_at), (parts,), jnp.float32, least / len(cuts), largest / len(cuts)))
        gain = gain * jnp.repeat(heights, shape[axis_at] // parts).reshape([-1 if axis == axis_at else 1 for axis in range(len(shape))])
    return gain


def noise(own_key, shape, deviation, bound, shards=(), kind=jnp.bfloat16):
    values = jax.random.normal(own_key, shape, jnp.float32) * deviation
    if len(shards) > 0:
        values = steps_of(own_key, shape, shards, -0.22, 0.18) * values
    return jnp.clip(values, min=-bound, max=bound).astype(kind)


def setup_inputs(seed: int = 0, part: int = 0) -> dict:
    streams_of = jax.random.split(jax.random.key(seed), 11)
    own_keys = jax.random.split(jax.random.fold_in(streams_of[10], part), 11)
    blocks = noise(own_keys[0], (STATES, TOTAL), 1.0, 6.0, ((0, 4), (1, 4)))
    boundary_shift = draw_boundary_shift(jax.random.fold_in(jax.random.fold_in(streams_of[10], part), 71), part)
    centre = jnp.clip(jax.random.uniform(own_keys[2], (N_CUTS,), jnp.float32, -1.0, 1.0) * steps_of(own_keys[2], (N_CUTS,), ((0, 4),), -0.4, 0.0), -1.0, 1.0)
    half_width = jnp.clip(1.0 + 1.0 * jax.random.uniform(own_keys[3], (N_CUTS,), jnp.float32) ** steps_of(own_keys[3], (N_CUTS,), ((0, 4),), -0.2, 0.2), 1.0, 2.0)
    cell_matrix = noise(streams_of[4], (CELL_NODES, CELL_NODES), CELL_NODES ** -0.5, 0.4375)
    cell_coef = jnp.clip(jnp.exp(math.log(1.5) - 1.60943787 * jax.random.uniform(own_keys[5], (CELLS,), jnp.float32) ** steps_of(own_keys[5], (CELLS,), ((0, 4),), -0.2, 0.2)), 0.3, 1.5)
    connectivity = place_ends(jax.random.randint(own_keys[6], (CELL_NODES, CELLS), 0, NODES_DEV + GHOST), jax.random.fold_in(own_keys[6], 1), 0, (NODES_DEV + GHOST) - 1).astype(jnp.int32)
    halo_list = draw_halo_list(jax.random.fold_in(jax.random.fold_in(streams_of[10], part), 71), part)
    mass = draw_mass(jax.random.fold_in(jax.random.fold_in(streams_of[10], part), 71), part)
    potential = jnp.clip(0.2 + 0.8 * jax.random.uniform(own_keys[9], (TOTAL,), jnp.float32) ** steps_of(own_keys[9], (TOTAL,), ((0, 4),), -0.2, 0.2), 0.2, 1.0)
    return {"blocks": blocks, "boundary_shift": boundary_shift, "centre": centre, "half_width": half_width, "cell_matrix": cell_matrix, "cell_coef": cell_coef, "connectivity": connectivity, "halo_list": halo_list, "mass": mass, "potential": potential}


def global_nodes(connectivity, halo_list):
    device_of = (jnp.arange(CELLS_DEV * N_MESH, dtype=jnp.int32) // CELLS_DEV)[None, :]
    owned = connectivity < NODES_DEV
    owner = device_of + 1
    ghost_index = jnp.clip(connectivity - NODES_DEV, 0, GHOST - 1)
    lookup = halo_list[jnp.clip(owner, 0, N_MESH - 1) * GHOST + ghost_index]
    ghost_global = jnp.where(owner < N_MESH, owner * NODES_DEV + lookup, TOTAL)
    return jnp.where(owned, device_of * NODES_DEV + connectivity, ghost_global).astype(jnp.int32)

def apply_operator(vec, nodes, cell_matrix, cell_coef, mass, potential):
    padded = jnp.concatenate([vec, jnp.zeros((vec.shape[0], 1), vec.dtype)], axis=1)
    values = padded[:, nodes].astype(jnp.float32)
    products = jnp.einsum('ij,vjc->vic', cell_matrix.astype(jnp.float32), values) * cell_coef
    summed = jnp.zeros((vec.shape[0], TOTAL + 1), jnp.float32).at[:, nodes].add(products)
    return summed[:, :TOTAL] / mass + potential * vec.astype(jnp.float32)

def reference(blocks, boundary_shift, centre, half_width, cell_matrix, cell_coef, connectivity, halo_list, mass, potential):
    nodes = global_nodes(connectivity, halo_list)
    empty = jnp.zeros((BLOCK, TOTAL), blocks.dtype)
    padded_blocks = jnp.concatenate([empty, blocks, empty], axis=0)

    def one_slice(slice_index):
        start = (slice_index * BLOCK + BLOCK + boundary_shift[slice_index]).astype(jnp.int32)
        window = lax.dynamic_slice_in_dim(padded_blocks, start, BLOCK, 0)
        middle = centre[slice_index]
        spread = half_width[slice_index]
        first = ((apply_operator(window, nodes, cell_matrix, cell_coef, mass, potential) - middle * window.astype(jnp.float32)) / spread).astype(jnp.bfloat16)
        second = 2.0 * (apply_operator(first, nodes, cell_matrix, cell_coef, mass, potential) - middle * first.astype(jnp.float32)) / spread - window.astype(jnp.float32)
        gram = jnp.dot(second * mass, second.T, precision=lax.Precision.HIGHEST) / TOTAL
        lower = jnp.linalg.cholesky(gram)
        return lax.linalg.triangular_solve(lower, second, left_side=True, lower=True)
    result = lax.map(one_slice, jnp.arange(N_CUTS, dtype=jnp.int32))
    return result.reshape(N_CUTS * BLOCK, TOTAL)
```

```python
import functools
import jax
import jax.numpy as jnp
from jax import lax
from jax.experimental import pallas as pl
from jax.experimental.pallas import tpu as pltpu
from jax.sharding import PartitionSpec as P

MESH = pl.DeviceIdType.MESH
F32, BF16 = jnp.float32, jnp.bfloat16
W = 256
UNROLL = 4
NT = (((1,), (1,)), ((), ()))
NN = (((1,), (0,)), ((), ()))


def dot(a, b, dims=NN, precision=None):
    return lax.dot_general(a, b, dims, precision=precision, preferred_element_type=F32)


def kernel(
    n_cuts, n_mesh,
    blocks, shift, centre, half_width, cell_matrix, coef, conn, halo, mass, potential,
    out,
    ext, win, fst, onehot, idx, group, kpad, acc, masked, ghost_out, ret, second, grams,
    cut_send, cut_recv, ghost_send, ghost_recv, ret_send, ret_recv, gram_send, gram_recv,
):
    rows, nodes = blocks.shape
    half = rows // 2
    cells = conn.shape[1]
    owned = nodes // W
    parts = owned + 1
    cut, me = lax.axis_index("cuts"), lax.axis_index("mesh")

    barrier = pltpu.get_barrier_semaphore()

    @pl.when(cut > 0)
    def _():
        pl.semaphore_signal(barrier, inc=1, device_id={"cuts": cut - 1}, device_id_type=MESH)

    @pl.when(cut < n_cuts - 1)
    def _():
        pl.semaphore_signal(barrier, inc=1, device_id={"cuts": cut + 1}, device_id_type=MESH)

    for step in range(1, n_mesh):
        pl.semaphore_signal(
            barrier, inc=1, device_id={"mesh": lax.rem(me + step, n_mesh)}, device_id_type=MESH
        )
    greeted = (n_mesh - 1) + jnp.where(cut > 0, 1, 0) + jnp.where(cut < n_cuts - 1, 1, 0)
    pl.semaphore_wait(barrier, greeted)

    def edge(up):
        return pltpu.make_async_remote_copy(
            src_ref=blocks.at[pl.ds(half if up else 0, half)],
            dst_ref=ext.at[pl.ds(0 if up else half + rows, half)],
            send_sem=cut_send.at[0 if up else 1],
            recv_sem=cut_recv.at[0 if up else 1],
            device_id={"cuts": jnp.clip(cut + (1 if up else -1), 0, n_cuts - 1)},
            device_id_type=MESH,
        )

    @pl.when(cut < n_cuts - 1)
    def _():
        edge(True).start()

    @pl.when(cut > 0)
    def _():
        edge(False).start()

    idx[...] = jnp.full(idx.shape, -1, jnp.int32)
    idx[0 : conn.shape[0], 0:cells] = conn[...]
    turned = jnp.transpose(idx[...])[0:cells]
    group[0:cells, :] = turned
    group[cells : cells + 1, :] = halo[...]

    kpad[...] = jnp.zeros(kpad.shape, F32)
    kpad[0 : conn.shape[0], 0 : conn.shape[0]] = cell_matrix[...].astype(F32)
    kmat = kpad[...].astype(BF16)

    place = lax.broadcasted_iota(jnp.int32, (W, W), 0)

    @pl.loop(0, cells + 1)
    def _(c):
        low = group[pl.ds(c, 1), :] & (W - 1)
        onehot[:, pl.ds(pl.multiple_of(c * W, W), W)] = jnp.where(place == low, 1.0, 0.0).astype(BF16)

    ext[half : half + rows, :] = blocks[...]

    @pl.when(me == n_mesh - 1)
    def _():
        win[owned * rows :, :] = jnp.zeros((rows, W), BF16)
        fst[owned * rows :, :] = jnp.zeros((rows, W), BF16)

    @pl.when(me == 0)
    def _():
        ret[...] = jnp.zeros(ret.shape, F32)

    @pl.when(cut > 0)
    def _():
        edge(True).wait_recv()

    @pl.when(cut == 0)
    def _():
        ext[0:half, :] = jnp.zeros((half, nodes), BF16)

    @pl.when(cut < n_cuts - 1)
    def _():
        edge(False).wait_recv()

    @pl.when(cut == n_cuts - 1)
    def _():
        ext[half + rows :, :] = jnp.zeros((half, nodes), BF16)

    pick = (
        lax.broadcasted_iota(jnp.int32, (rows, 2 * rows), 1)
        == lax.broadcasted_iota(jnp.int32, (rows, 2 * rows), 0) + (half + shift[0])
    )
    pick = jnp.where(pick, 1.0, 0.0).astype(BF16)
    for k in range(owned):
        win[k * rows : (k + 1) * rows, :] = dot(pick, ext[:, k * W : (k + 1) * W]).astype(BF16)

    middle, scale = centre[0], 1.0 / half_width[0]

    def gathered(v, c, count):
        found = dot(v[0 : count * rows, :], onehot[:, pl.ds(pl.multiple_of(c * W, W), W)])
        high = jnp.broadcast_to(group[pl.ds(c, 1), :] >> 8, (rows, W))
        total = jnp.zeros((rows, W), F32)
        for k in range(count):
            total = jnp.where(high == k, found[k * rows : (k + 1) * rows], total)
        return total, high

    def spread(value, high, count, split, at):
        kinds = [value]
        if split:
            kinds.append(value - value.astype(BF16).astype(F32))
        for kind, part in enumerate(kinds):
            for k in range(count):
                row = (kind * count + k) * rows
                masked[row : row + rows, at : at + W] = jnp.where(high == k, part, 0.0).astype(BF16)

    def summed(c, width, count, split):
        places = onehot[:, pl.ds(pl.multiple_of(c * W, W), width)]
        height = count * rows
        total = dot(masked[0:height, 0:width], places, NT)
        if split:
            total += dot(masked[height : 2 * height, 0:width], places, NT)
        return total

    def apply_cells(v, at, split):
        def ghost():
            return pltpu.make_async_remote_copy(
                src_ref=ghost_out.at[at],
                dst_ref=v.at[pl.ds(owned * rows, rows)],
                send_sem=ghost_send.at[at],
                recv_sem=ghost_recv.at[at],
                device_id={"mesh": jnp.maximum(me - 1, 0)},
                device_id_type=MESH,
            )

        def back():
            return pltpu.make_async_remote_copy(
                src_ref=acc.at[at, pl.ds(owned * rows, rows)],
                dst_ref=ret.at[at],
                send_sem=ret_send.at[at],
                recv_sem=ret_recv.at[at],
                device_id={"mesh": jnp.minimum(me + 1, n_mesh - 1)},
                device_id_type=MESH,
            )

        ghost_out[at] = gathered(v, cells, owned)[0].astype(BF16)

        @pl.when(me > 0)
        def _():
            ghost().start()

        acc[at] = jnp.zeros(acc.shape[1:], F32)

        @pl.when(me < n_mesh - 1)
        def _():
            ghost().wait_recv()

        @pl.loop(0, cells // UNROLL)
        def _(step):
            for u in range(UNROLL):
                c = step * UNROLL + u
                values, high = gathered(v, c, parts)
                products = dot(values.astype(BF16), kmat, NT) * coef[c]
                spread(products, high, parts, split, u * W)
            acc[at] += summed(step * UNROLL, UNROLL * W, parts, split)

        @pl.when(me < n_mesh - 1)
        def _():
            back().start()

        @pl.when(me > 0)
        def _():
            back().wait_recv()

        high = jnp.broadcast_to(group[cells : cells + 1, :] >> 8, (rows, W))
        spread(ret[at], high, owned, True, 0)
        acc[at, 0 : owned * rows, :] += summed(cells, W, owned, True)

        @pl.when(me > 0)
        def _():
            ghost().wait_send()

        @pl.when(me < n_mesh - 1)
        def _():
            back().wait_send()

    def operated(v, at, k):
        own = slice(k * rows, (k + 1) * rows)
        cols = slice(k * W, (k + 1) * W)
        return (
            acc[at, own, :] / mass[:, cols] + (potential[:, cols] - middle) * v[own, :].astype(F32)
        ) * scale

    apply_cells(win, 0, True)
    for k in range(owned):
        fst[k * rows : (k + 1) * rows, :] = operated(win, 0, k).astype(BF16)
    apply_cells(fst, 1, False)
    partial = jnp.zeros((rows, rows), F32)
    for k in range(owned):
        cols = slice(k * W, (k + 1) * W)
        piece = 2.0 * operated(fst, 1, k) - win[k * rows : (k + 1) * rows, :].astype(F32)
        second[:, cols] = piece
        partial += dot(piece * mass[:, cols], piece, NT, lax.Precision.HIGHEST)
    partial = partial / (nodes * n_mesh)
    grams[pl.ds(me, 1)] = jnp.concatenate([partial, jnp.zeros((rows, rows), F32)], axis=1)[None]

    def share(step):
        return pltpu.make_async_remote_copy(
            src_ref=grams.at[me],
            dst_ref=grams.at[me],
            send_sem=gram_send.at[step],
            recv_sem=gram_recv.at[step],
            device_id={"mesh": lax.rem(me + step, n_mesh)},
            device_id_type=MESH,
        )

    for step in range(1, n_mesh):
        share(step).start()
    for step in range(1, n_mesh):
        share(step).wait_recv()

    work = grams[0]
    for i in range(1, n_mesh):
        work += grams[i]
    line = lax.broadcasted_iota(jnp.int32, (rows, 2 * rows), 0)
    lane = lax.broadcasted_iota(jnp.int32, (rows, 2 * rows), 1)
    work = jnp.where(lane == line + rows, 1.0, work)
    for k in range(rows):
        pivot_row = work[k : k + 1, :]
        column = work[:, k : k + 1]
        pivot = work[k : k + 1, k : k + 1]
        factor = jnp.where(line[:, 0:1] > k, column / pivot, 0.0)
        work = work - factor * pivot_row
    diagonal = jnp.sum(jnp.where(line == lane, work, 0.0), axis=1, keepdims=True)
    inverse = work[:, rows:] / jnp.sqrt(diagonal)
    for k in range(owned):
        cols = slice(k * W, (k + 1) * W)
        out[:, cols] = dot(inverse, second[:, cols], NN, lax.Precision.HIGHEST)

    for step in range(1, n_mesh):
        share(step).wait_send()

    @pl.when(cut < n_cuts - 1)
    def _():
        edge(True).wait_send()

    @pl.when(cut > 0)
    def _():
        edge(False).wait_send()


def body(
    blocks, boundary_shift, centre, half_width, cell_matrix, cell_coef, connectivity, halo_list,
    mass, potential,
):
    n_cuts, n_mesh = lax.axis_size("cuts"), lax.axis_size("mesh")
    rows, nodes = blocks.shape
    cells = connectivity.shape[1]
    parts = nodes // W + 1
    vmem = pl.BlockSpec(memory_space=pltpu.VMEM)
    smem = pl.BlockSpec(memory_space=pltpu.SMEM)
    dma = pltpu.SemaphoreType.DMA
    return pl.pallas_call(
        functools.partial(kernel, n_cuts, n_mesh),
        out_shape=jax.ShapeDtypeStruct((rows, nodes), F32),
        in_specs=[vmem, smem, smem, smem, vmem, smem, vmem, vmem, vmem, vmem],
        out_specs=vmem,
        scratch_shapes=[
            pltpu.VMEM((2 * rows, nodes), BF16),
            pltpu.VMEM((parts * rows, W), BF16),
            pltpu.VMEM((parts * rows, W), BF16),
            pltpu.VMEM((W, (cells + 1) * W), BF16),
            pltpu.VMEM((W, 128), jnp.int32),
            pltpu.VMEM((cells + 8, W), jnp.int32),
            pltpu.VMEM((W, W), F32),
            pltpu.VMEM((2, parts * rows, W), F32),
            pltpu.VMEM((2 * parts * rows, UNROLL * W), BF16),
            pltpu.VMEM((2, rows, W), BF16),
            pltpu.VMEM((2, rows, W), F32),
            pltpu.VMEM((rows, nodes), F32),
            pltpu.VMEM((n_mesh, rows, 2 * rows), F32),
            dma((2,)), dma((2,)), dma((2,)), dma((2,)), dma((2,)), dma((2,)),
            dma((n_mesh,)), dma((n_mesh,)),
        ],
        compiler_params=pltpu.CompilerParams(
            collective_id=0, has_side_effects=True, vmem_limit_bytes=48 * 1024 * 1024
        ),
    )(
        blocks, boundary_shift, centre, half_width, cell_matrix, cell_coef, connectivity,
        halo_list.reshape(1, -1), mass.reshape(1, -1), potential.reshape(1, -1),
    )


def solution(mesh):
    return jax.shard_map(
        body,
        mesh=mesh,
        in_specs=(
            P(("job", "cuts"), "mesh"),
            P(("job", "cuts")),
            P(("job", "cuts")),
            P(("job", "cuts")),
            P(),
            P(("job", "mesh")),
            P(None, ("job", "mesh")),
            P(("job", "mesh")),
            P(("job", "mesh")),
            P(("job", "mesh")),
        ),
        out_specs=P(("job", "cuts"), "mesh"),
        check_vma=False,
    )
```

```python
import functools
import jax
import jax.numpy as jnp
from jax import lax
from jax.experimental import pallas as pl
from jax.experimental.pallas import tpu as pltpu
from jax.sharding import PartitionSpec as P

MESH = pl.DeviceIdType.MESH
F32, BF16 = jnp.float32, jnp.bfloat16
W = 256
UNROLL = 8
PIVOTS = 4
NT = (((1,), (1,)), ((), ()))
NN = (((1,), (0,)), ((), ()))


def dot(a, b, dims=NN, precision=None):
    return lax.dot_general(a, b, dims, precision=precision, preferred_element_type=F32)


def kernel(
    n_cuts, n_mesh,
    blocks, shift, centre, half_width, cell_matrix, coef, conn, halo, mass, potential,
    out,
    ext, win, fst, onehot, idx, group, kpad, acc, masked, vals, prods, ghost_out, back_out, ret, second, grams,
    cut_send, cut_recv, ghost_send, ghost_recv, ret_send, ret_recv, gram_send, gram_recv,
):
    rows, nodes = blocks.shape
    half = rows // 2
    cells = conn.shape[1]
    owned = nodes // W
    cut, me = lax.axis_index("cuts"), lax.axis_index("mesh")

    barrier = pltpu.get_barrier_semaphore()

    @pl.when(cut > 0)
    def _():
        pl.semaphore_signal(barrier, inc=1, device_id={"cuts": cut - 1}, device_id_type=MESH)

    @pl.when(cut < n_cuts - 1)
    def _():
        pl.semaphore_signal(barrier, inc=1, device_id={"cuts": cut + 1}, device_id_type=MESH)

    for step in range(1, n_mesh):
        pl.semaphore_signal(
            barrier, inc=1, device_id={"mesh": lax.rem(me + step, n_mesh)}, device_id_type=MESH
        )
    greeted = (n_mesh - 1) + jnp.where(cut > 0, 1, 0) + jnp.where(cut < n_cuts - 1, 1, 0)
    pl.semaphore_wait(barrier, greeted)

    def edge(up):
        return pltpu.make_async_remote_copy(
            src_ref=blocks.at[pl.ds(half if up else 0, half)],
            dst_ref=ext.at[pl.ds(0 if up else half + rows, half)],
            send_sem=cut_send.at[0 if up else 1],
            recv_sem=cut_recv.at[0 if up else 1],
            device_id={"cuts": jnp.clip(cut + (1 if up else -1), 0, n_cuts - 1)},
            device_id_type=MESH,
        )

    @pl.when(cut < n_cuts - 1)
    def _():
        edge(True).start()

    @pl.when(cut > 0)
    def _():
        edge(False).start()

    idx[...] = jnp.full(idx.shape, -1, jnp.int32)
    idx[0 : conn.shape[0], 0:cells] = conn[...]
    turned = jnp.transpose(idx[...])[0:cells]
    group[0:cells, :] = turned
    group[cells : cells + 1, :] = halo[...]

    kpad[...] = jnp.zeros(kpad.shape, F32)
    kpad[0 : conn.shape[0], 0 : conn.shape[0]] = cell_matrix[...].astype(F32)
    kmat = jnp.transpose(kpad[...]).astype(BF16)

    place = lax.broadcasted_iota(jnp.int32, (W, W), 0)

    @pl.loop(0, cells + 1)
    def _(c):
        low = group[pl.ds(c, 1), :] & (W - 1)
        onehot[:, pl.ds(pl.multiple_of(c * W, W), W)] = jnp.where(place == low, 1.0, 0.0).astype(BF16)

    ext[half : half + rows, :] = blocks[...]

    @pl.when(me == n_mesh - 1)
    def _():
        win[owned * rows :, :] = jnp.zeros((rows, W), BF16)
        fst[owned * rows :, :] = jnp.zeros((rows, W), BF16)

    @pl.when(me == 0)
    def _():
        ret[...] = jnp.zeros(ret.shape, F32)

    @pl.when(cut > 0)
    def _():
        edge(True).wait_recv()

    @pl.when(cut == 0)
    def _():
        ext[0:half, :] = jnp.zeros((half, nodes), BF16)

    @pl.when(cut < n_cuts - 1)
    def _():
        edge(False).wait_recv()

    @pl.when(cut == n_cuts - 1)
    def _():
        ext[half + rows :, :] = jnp.zeros((half, nodes), BF16)

    pick = (
        lax.broadcasted_iota(jnp.int32, (rows, 2 * rows), 1)
        == lax.broadcasted_iota(jnp.int32, (rows, 2 * rows), 0) + (half + shift[0])
    )
    pick = jnp.where(pick, 1.0, 0.0).astype(BF16)
    for k in range(owned):
        win[k * rows : (k + 1) * rows, :] = dot(pick, ext[:, k * W : (k + 1) * W]).astype(BF16)

    middle, scale = centre[0], 1.0 / half_width[0]

    def tile(c, width=W):
        return onehot[:, pl.ds(pl.multiple_of(c * W, W), width)]

    def high_of(c):
        return jnp.broadcast_to(group[pl.ds(c, 1), :] >> 8, (rows, W))

    def gathered(v, c):
        found = dot(v[0 : owned * rows, :], tile(c))
        high = high_of(c)
        total = jnp.zeros((rows, W), F32)
        for k in range(owned):
            total = jnp.where(high == k, found[k * rows : (k + 1) * rows], total)
        return total.astype(BF16)

    def kinds_of(value, split):
        if not split:
            return [value]
        return [value, value - value.astype(BF16).astype(F32)]

    def spread(value, high, split, at):
        for kind, part in enumerate(kinds_of(value, split)):
            for k in range(owned):
                row = (kind * owned + k) * rows
                masked[row : row + rows, at : at + W] = jnp.where(high == k, part, 0.0).astype(BF16)

    def summed(c, width, split):
        height = owned * rows
        total = dot(masked[0:height, 0:width], tile(c, width), NT)
        if split:
            total += dot(masked[height : 2 * height, 0:width], tile(c, width), NT)
        return total

    def apply_cells(v, at, split):
        def ghost():
            return pltpu.make_async_remote_copy(
                src_ref=ghost_out.at[at],
                dst_ref=v.at[pl.ds(owned * rows, rows)],
                send_sem=ghost_send.at[at],
                recv_sem=ghost_recv.at[at],
                device_id={"mesh": jnp.maximum(me - 1, 0)},
                device_id_type=MESH,
            )

        def back():
            return pltpu.make_async_remote_copy(
                src_ref=back_out.at[at],
                dst_ref=ret.at[at],
                send_sem=ret_send.at[at],
                recv_sem=ret_recv.at[at],
                device_id={"mesh": jnp.minimum(me + 1, n_mesh - 1)},
                device_id_type=MESH,
            )

        ghost_out[at] = gathered(v, cells)

        @pl.when(me > 0)
        def _():
            ghost().start()

        @pl.loop(0, cells // UNROLL)
        def _(step):
            for u in range(UNROLL):
                c = step * UNROLL + u
                vals[pl.ds(pl.multiple_of(c * rows, rows), rows), :] = gathered(v, c)

        acc[...] = jnp.zeros(acc.shape, F32)
        back_out[at] = jnp.zeros((rows, W), F32)

        @pl.when(me < n_mesh - 1)
        def _():
            ghost().wait_recv()

        @pl.loop(0, cells // UNROLL)
        def _(step):
            base = pl.multiple_of(step * (UNROLL * rows), UNROLL * rows)
            outer = v[owned * rows :, :]
            full = []
            for u in range(UNROLL):
                c = step * UNROLL + u
                found = dot(outer, tile(c))
                own = vals[pl.ds(pl.multiple_of(c * rows, rows), rows), :].astype(F32)
                full.append(jnp.where(high_of(c) == owned, found, own).astype(BF16))
            results = dot(jnp.concatenate(full, axis=0), kmat)
            sums = jnp.zeros((rows, W), F32)
            lefts = []
            for u in range(UNROLL):
                c = step * UNROLL + u
                product = results[u * rows : (u + 1) * rows] * coef[c]
                prods[pl.ds(pl.multiple_of(c * rows, rows), rows), :] = product
                edge_part = jnp.where(high_of(c) == owned, product, 0.0)
                lefts.append(
                    jnp.concatenate([p.astype(BF16) for p in kinds_of(edge_part, split)], axis=0)
                )
            both = dot(jnp.concatenate(lefts, axis=1), tile(step * UNROLL, UNROLL * W), NT)
            sums = both[0:rows] + both[rows:] if split else both
            back_out[at] += sums

        @pl.when(me < n_mesh - 1)
        def _():
            back().start()

        @pl.loop(0, cells // UNROLL)
        def _(step):
            for u in range(UNROLL):
                c = step * UNROLL + u
                product = prods[pl.ds(pl.multiple_of(c * rows, rows), rows), :]
                spread(product, high_of(c), split, u * W)
            acc[...] += summed(step * UNROLL, UNROLL * W, split)

        @pl.when(me > 0)
        def _():
            back().wait_recv()

        spread(ret[at], high_of(cells), True, 0)
        acc[...] += summed(cells, W, True)

        @pl.when(me > 0)
        def _():
            ghost().wait_send()

        @pl.when(me < n_mesh - 1)
        def _():
            back().wait_send()

    def operated(v, at, k):
        own = slice(k * rows, (k + 1) * rows)
        cols = slice(k * W, (k + 1) * W)
        return (
            acc[own, :] / mass[:, cols] + (potential[:, cols] - middle) * v[own, :].astype(F32)
        ) * scale

    apply_cells(win, 0, True)
    for k in range(owned):
        fst[k * rows : (k + 1) * rows, :] = operated(win, 0, k).astype(BF16)
    apply_cells(fst, 1, False)
    partial = jnp.zeros((rows, rows), F32)
    for k in range(owned):
        cols = slice(k * W, (k + 1) * W)
        piece = 2.0 * operated(fst, 1, k) - win[k * rows : (k + 1) * rows, :].astype(F32)
        second[:, cols] = piece
        partial += dot(piece * mass[:, cols], piece, NT, lax.Precision.HIGHEST)
    partial = partial / (nodes * n_mesh)
    grams[pl.ds(me, 1)] = jnp.concatenate([partial, jnp.zeros((rows, rows), F32)], axis=1)[None]

    def share(step):
        return pltpu.make_async_remote_copy(
            src_ref=grams.at[me],
            dst_ref=grams.at[me],
            send_sem=gram_send.at[step],
            recv_sem=gram_recv.at[step],
            device_id={"mesh": lax.rem(me + step, n_mesh)},
            device_id_type=MESH,
        )

    for step in range(1, n_mesh):
        share(step).start()
    for step in range(1, n_mesh):
        share(step).wait_recv()

    work = grams[0]
    for i in range(1, n_mesh):
        work += grams[i]
    line = lax.broadcasted_iota(jnp.int32, (rows, 2 * rows), 0)
    lane = lax.broadcasted_iota(jnp.int32, (rows, 2 * rows), 1)
    work = jnp.where(lane == line + rows, 1.0, work)
    for first in range(0, rows, PIVOTS):
        columns = [
            jnp.broadcast_to(work[:, first + j : first + j + 1], work.shape) for j in range(PIVOTS)
        ]
        lines = [work[first + j : first + j + 1, :] for j in range(PIVOTS)]
        for j in range(PIVOTS):
            at = first + j
            inverse_pivot = 1.0 / columns[j][at : at + 1, :]
            scaled = lines[j] * inverse_pivot
            for i in range(j + 1, PIVOTS):
                entry = columns[j][first + i : first + i + 1, :]
                columns[i] = columns[i] - columns[j] * (entry * inverse_pivot)
                lines[i] = lines[i] - entry * scaled
            work = work - jnp.where(line > at, columns[j], 0.0) * scaled
    diagonal = jnp.sum(jnp.where(line == lane, work, 0.0), axis=1, keepdims=True)
    inverse = work[:, rows:] / jnp.sqrt(diagonal)
    rough = inverse.astype(BF16).astype(F32)
    left = jnp.concatenate([rough, rough, inverse - rough], axis=1).astype(BF16)
    for k in range(owned):
        cols = slice(k * W, (k + 1) * W)
        upper = second[:, cols].astype(BF16)
        rest = (second[:, cols] - upper.astype(F32)).astype(BF16)
        out[:, cols] = dot(left, jnp.concatenate([upper, rest, upper], axis=0))

    for step in range(1, n_mesh):
        share(step).wait_send()

    @pl.when(cut < n_cuts - 1)
    def _():
        edge(True).wait_send()

    @pl.when(cut > 0)
    def _():
        edge(False).wait_send()


def body(
    blocks, boundary_shift, centre, half_width, cell_matrix, cell_coef, connectivity, halo_list,
    mass, potential,
):
    n_cuts, n_mesh = lax.axis_size("cuts"), lax.axis_size("mesh")
    rows, nodes = blocks.shape
    cells = connectivity.shape[1]
    parts = nodes // W + 1
    vmem = pl.BlockSpec(memory_space=pltpu.VMEM)
    smem = pl.BlockSpec(memory_space=pltpu.SMEM)
    dma = pltpu.SemaphoreType.DMA
    return pl.pallas_call(
        functools.partial(kernel, n_cuts, n_mesh),
        out_shape=jax.ShapeDtypeStruct((rows, nodes), F32),
        in_specs=[vmem, smem, smem, smem, vmem, smem, vmem, vmem, vmem, vmem],
        out_specs=vmem,
        scratch_shapes=[
            pltpu.VMEM((2 * rows, nodes), BF16),
            pltpu.VMEM((parts * rows, W), BF16),
            pltpu.VMEM((parts * rows, W), BF16),
            pltpu.VMEM((W, (cells + 1) * W), BF16),
            pltpu.VMEM((W, 128), jnp.int32),
            pltpu.VMEM((cells + 8, W), jnp.int32),
            pltpu.VMEM((W, W), F32),
            pltpu.VMEM(((parts - 1) * rows, W), F32),
            pltpu.VMEM((2 * (parts - 1) * rows, UNROLL * W), BF16),
            pltpu.VMEM((cells * rows, W), BF16),
            pltpu.VMEM((cells * rows, W), F32),
            pltpu.VMEM((2, rows, W), BF16),
            pltpu.VMEM((2, rows, W), F32),
            pltpu.VMEM((2, rows, W), F32),
            pltpu.VMEM((rows, nodes), F32),
            pltpu.VMEM((n_mesh, rows, 2 * rows), F32),
            dma((2,)), dma((2,)), dma((2,)), dma((2,)), dma((2,)), dma((2,)),
            dma((n_mesh,)), dma((n_mesh,)),
        ],
        compiler_params=pltpu.CompilerParams(
            collective_id=0, has_side_effects=True, vmem_limit_bytes=48 * 1024 * 1024
        ),
    )(
        blocks, boundary_shift, centre, half_width, cell_matrix, cell_coef, connectivity,
        halo_list.reshape(1, -1), mass.reshape(1, -1), potential.reshape(1, -1),
    )


def solution(mesh):
    return jax.shard_map(
        body,
        mesh=mesh,
        in_specs=(
            P(("job", "cuts"), "mesh"),
            P(("job", "cuts")),
            P(("job", "cuts")),
            P(("job", "cuts")),
            P(),
            P(("job", "mesh")),
            P(None, ("job", "mesh")),
            P(("job", "mesh")),
            P(("job", "mesh")),
            P(("job", "mesh")),
        ),
        out_specs=P(("job", "cuts"), "mesh"),
        check_vma=False,
    )
```

```python
import functools
import jax
import jax.numpy as jnp
from jax import lax
from jax.experimental import pallas as pl
from jax.experimental.pallas import tpu as pltpu
from jax.sharding import PartitionSpec as P

MESH = pl.DeviceIdType.MESH
F32, BF16 = jnp.float32, jnp.bfloat16
W = 256
UNROLL = 16
PIVOTS = 8
NT = (((1,), (1,)), ((), ()))
NN = (((1,), (0,)), ((), ()))


def dot(a, b, dims=NN, precision=None):
    return lax.dot_general(a, b, dims, precision=precision, preferred_element_type=F32)


def kernel(
    n_cuts, n_mesh,
    blocks, shift, centre, half_width, cell_matrix, coef, conn, halo, mass, potential,
    out,
    ext, win, fst, onehot, idx, group, kpad, acc, masked, vals, prods, ghost_out, back_out, ret, second, grams,
    cut_send, cut_recv, ghost_send, ghost_recv, ret_send, ret_recv, gram_send, gram_recv,
):
    rows, nodes = blocks.shape
    half = rows // 2
    cells = conn.shape[1]
    owned = nodes // W
    cut, me = lax.axis_index("cuts"), lax.axis_index("mesh")

    barrier = pltpu.get_barrier_semaphore()

    @pl.when(cut > 0)
    def _():
        pl.semaphore_signal(barrier, inc=1, device_id={"cuts": cut - 1}, device_id_type=MESH)

    @pl.when(cut < n_cuts - 1)
    def _():
        pl.semaphore_signal(barrier, inc=1, device_id={"cuts": cut + 1}, device_id_type=MESH)

    for step in range(1, n_mesh):
        pl.semaphore_signal(
            barrier, inc=1, device_id={"mesh": lax.rem(me + step, n_mesh)}, device_id_type=MESH
        )
    greeted = (n_mesh - 1) + jnp.where(cut > 0, 1, 0) + jnp.where(cut < n_cuts - 1, 1, 0)
    pl.semaphore_wait(barrier, greeted)

    def edge(up):
        return pltpu.make_async_remote_copy(
            src_ref=blocks.at[pl.ds(half if up else 0, half)],
            dst_ref=ext.at[pl.ds(0 if up else half + rows, half)],
            send_sem=cut_send.at[0 if up else 1],
            recv_sem=cut_recv.at[0 if up else 1],
            device_id={"cuts": jnp.clip(cut + (1 if up else -1), 0, n_cuts - 1)},
            device_id_type=MESH,
        )

    @pl.when(cut < n_cuts - 1)
    def _():
        edge(True).start()

    @pl.when(cut > 0)
    def _():
        edge(False).start()

    idx[...] = jnp.full(idx.shape, -1, jnp.int32)
    idx[0 : conn.shape[0], 0:cells] = conn[...]
    turned = jnp.transpose(idx[...])[0:cells]
    group[0:cells, :] = turned
    group[cells : cells + 1, :] = halo[...]

    kpad[...] = jnp.zeros(kpad.shape, F32)
    kpad[0 : conn.shape[0], 0 : conn.shape[0]] = cell_matrix[...].astype(F32)
    kmat = jnp.transpose(kpad[...]).astype(BF16)

    place = lax.broadcasted_iota(jnp.int32, (W, W), 0)

    @pl.loop(0, cells + 1)
    def _(c):
        low = group[pl.ds(c, 1), :] & (W - 1)
        onehot[:, pl.ds(pl.multiple_of(c * W, W), W)] = jnp.where(place == low, 1.0, 0.0).astype(BF16)

    ext[half : half + rows, :] = blocks[...]

    @pl.when(me == n_mesh - 1)
    def _():
        win[owned * rows :, :] = jnp.zeros((rows, W), BF16)
        fst[owned * rows :, :] = jnp.zeros((rows, W), BF16)

    @pl.when(me == 0)
    def _():
        ret[...] = jnp.zeros(ret.shape, F32)

    @pl.when(cut > 0)
    def _():
        edge(True).wait_recv()

    @pl.when(cut == 0)
    def _():
        ext[0:half, :] = jnp.zeros((half, nodes), BF16)

    @pl.when(cut < n_cuts - 1)
    def _():
        edge(False).wait_recv()

    @pl.when(cut == n_cuts - 1)
    def _():
        ext[half + rows :, :] = jnp.zeros((half, nodes), BF16)

    pick = (
        lax.broadcasted_iota(jnp.int32, (rows, 2 * rows), 1)
        == lax.broadcasted_iota(jnp.int32, (rows, 2 * rows), 0) + (half + shift[0])
    )
    pick = jnp.where(pick, 1.0, 0.0).astype(BF16)
    for k in range(owned):
        win[k * rows : (k + 1) * rows, :] = dot(pick, ext[:, k * W : (k + 1) * W]).astype(BF16)

    middle, scale = centre[0], 1.0 / half_width[0]

    def tile(c, width=W):
        return onehot[:, pl.ds(pl.multiple_of(c * W, W), width)]

    def high_of(c):
        return jnp.broadcast_to(group[pl.ds(c, 1), :] >> 8, (rows, W))

    def gathered(v, c):
        found = dot(v[0 : owned * rows, :], tile(c))
        high = high_of(c)
        total = jnp.zeros((rows, W), F32)
        for k in range(owned):
            total = jnp.where(high == k, found[k * rows : (k + 1) * rows], total)
        return total.astype(BF16)

    def kinds_of(value, split):
        if not split:
            return [value]
        return [value, value - value.astype(BF16).astype(F32)]

    def spread(value, high, split, at):
        for kind, part in enumerate(kinds_of(value, split)):
            for k in range(owned):
                row = (kind * owned + k) * rows
                masked[row : row + rows, at : at + W] = jnp.where(high == k, part, 0.0).astype(BF16)

    def summed(c, width, split):
        height = owned * rows
        total = dot(masked[0:height, 0:width], tile(c, width), NT)
        if split:
            total += dot(masked[height : 2 * height, 0:width], tile(c, width), NT)
        return total

    def apply_cells(v, at, split):
        def ghost():
            return pltpu.make_async_remote_copy(
                src_ref=ghost_out.at[at],
                dst_ref=v.at[pl.ds(owned * rows, rows)],
                send_sem=ghost_send.at[at],
                recv_sem=ghost_recv.at[at],
                device_id={"mesh": jnp.maximum(me - 1, 0)},
                device_id_type=MESH,
            )

        def back():
            return pltpu.make_async_remote_copy(
                src_ref=back_out.at[at],
                dst_ref=ret.at[at],
                send_sem=ret_send.at[at],
                recv_sem=ret_recv.at[at],
                device_id={"mesh": jnp.minimum(me + 1, n_mesh - 1)},
                device_id_type=MESH,
            )

        ghost_out[at] = gathered(v, cells)

        @pl.when(me > 0)
        def _():
            ghost().start()

        @pl.loop(0, cells // UNROLL)
        def _(step):
            for u in range(UNROLL):
                c = step * UNROLL + u
                vals[pl.ds(pl.multiple_of(c * rows, rows), rows), :] = gathered(v, c)

        acc[...] = jnp.zeros(acc.shape, F32)
        back_out[at] = jnp.zeros((rows, W), F32)

        @pl.when(me < n_mesh - 1)
        def _():
            ghost().wait_recv()

        @pl.loop(0, cells // UNROLL)
        def _(step):
            base = pl.multiple_of(step * (UNROLL * rows), UNROLL * rows)
            outer = v[owned * rows :, :]
            full = []
            for u in range(UNROLL):
                c = step * UNROLL + u
                found = dot(outer, tile(c))
                own = vals[pl.ds(pl.multiple_of(c * rows, rows), rows), :].astype(F32)
                full.append(jnp.where(high_of(c) == owned, found, own).astype(BF16))
            results = dot(jnp.concatenate(full, axis=0), kmat)
            sums = jnp.zeros((rows, W), F32)
            lefts = []
            for u in range(UNROLL):
                c = step * UNROLL + u
                product = results[u * rows : (u + 1) * rows] * coef[c]
                prods[pl.ds(pl.multiple_of(c * rows, rows), rows), :] = product
                edge_part = jnp.where(high_of(c) == owned, product, 0.0)
                lefts.append(
                    jnp.concatenate([p.astype(BF16) for p in kinds_of(edge_part, split)], axis=0)
                )
            both = dot(jnp.concatenate(lefts, axis=1), tile(step * UNROLL, UNROLL * W), NT)
            sums = both[0:rows] + both[rows:] if split else both
            back_out[at] += sums

        @pl.when(me < n_mesh - 1)
        def _():
            back().start()

        @pl.loop(0, cells // UNROLL)
        def _(step):
            for u in range(UNROLL):
                c = step * UNROLL + u
                product = prods[pl.ds(pl.multiple_of(c * rows, rows), rows), :]
                spread(product, high_of(c), split, u * W)
            acc[...] += summed(step * UNROLL, UNROLL * W, split)

        @pl.when(me > 0)
        def _():
            back().wait_recv()

        spread(ret[at], high_of(cells), True, 0)
        acc[...] += summed(cells, W, True)

        @pl.when(me > 0)
        def _():
            ghost().wait_send()

        @pl.when(me < n_mesh - 1)
        def _():
            back().wait_send()

    def operated(v, at, k):
        own = slice(k * rows, (k + 1) * rows)
        cols = slice(k * W, (k + 1) * W)
        return (
            acc[own, :] / mass[:, cols] + (potential[:, cols] - middle) * v[own, :].astype(F32)
        ) * scale

    apply_cells(win, 0, True)
    for k in range(owned):
        fst[k * rows : (k + 1) * rows, :] = operated(win, 0, k).astype(BF16)
    apply_cells(fst, 1, False)
    partial = jnp.zeros((rows, rows), F32)
    for k in range(owned):
        cols = slice(k * W, (k + 1) * W)
        piece = 2.0 * operated(fst, 1, k) - win[k * rows : (k + 1) * rows, :].astype(F32)
        second[:, cols] = piece
        partial += dot(piece * mass[:, cols], piece, NT, lax.Precision.HIGHEST)
    partial = partial / (nodes * n_mesh)
    grams[pl.ds(me, 1)] = jnp.concatenate([partial, jnp.zeros((rows, rows), F32)], axis=1)[None]

    def share(step):
        return pltpu.make_async_remote_copy(
            src_ref=grams.at[me],
            dst_ref=grams.at[me],
            send_sem=gram_send.at[step],
            recv_sem=gram_recv.at[step],
            device_id={"mesh": lax.rem(me + step, n_mesh)},
            device_id_type=MESH,
        )

    for step in range(1, n_mesh):
        share(step).start()
    for step in range(1, n_mesh):
        share(step).wait_recv()

    work = grams[0]
    for i in range(1, n_mesh):
        work += grams[i]
    line = lax.broadcasted_iota(jnp.int32, (rows, 2 * rows), 0)
    lane = lax.broadcasted_iota(jnp.int32, (rows, 2 * rows), 1)
    work = jnp.where(lane == line + rows, 1.0, work)
    for first in range(0, rows, PIVOTS):
        columns = [
            jnp.broadcast_to(work[:, first + j : first + j + 1], work.shape) for j in range(PIVOTS)
        ]
        lines = [work[first + j : first + j + 1, :] for j in range(PIVOTS)]
        for j in range(PIVOTS):
            at = first + j
            inverse_pivot = 1.0 / columns[j][at : at + 1, :]
            scaled = lines[j] * inverse_pivot
            for i in range(j + 1, PIVOTS):
                entry = columns[j][first + i : first + i + 1, :]
                columns[i] = columns[i] - columns[j] * (entry * inverse_pivot)
                lines[i] = lines[i] - entry * scaled
            work = work - jnp.where(line > at, columns[j], 0.0) * scaled
    diagonal = jnp.sum(jnp.where(line == lane, work, 0.0), axis=1, keepdims=True)
    inverse = work[:, rows:] / jnp.sqrt(diagonal)
    rough = inverse.astype(BF16).astype(F32)
    left = jnp.concatenate([rough, rough, inverse - rough], axis=1).astype(BF16)
    for k in range(owned):
        cols = slice(k * W, (k + 1) * W)
        upper = second[:, cols].astype(BF16)
        rest = (second[:, cols] - upper.astype(F32)).astype(BF16)
        out[:, cols] = dot(left, jnp.concatenate([upper, rest, upper], axis=0))

    for step in range(1, n_mesh):
        share(step).wait_send()

    @pl.when(cut < n_cuts - 1)
    def _():
        edge(True).wait_send()

    @pl.when(cut > 0)
    def _():
        edge(False).wait_send()


def body(
    blocks, boundary_shift, centre, half_width, cell_matrix, cell_coef, connectivity, halo_list,
    mass, potential,
):
    n_cuts, n_mesh = lax.axis_size("cuts"), lax.axis_size("mesh")
    rows, nodes = blocks.shape
    cells = connectivity.shape[1]
    parts = nodes // W + 1
    vmem = pl.BlockSpec(memory_space=pltpu.VMEM)
    smem = pl.BlockSpec(memory_space=pltpu.SMEM)
    dma = pltpu.SemaphoreType.DMA
    return pl.pallas_call(
        functools.partial(kernel, n_cuts, n_mesh),
        out_shape=jax.ShapeDtypeStruct((rows, nodes), F32),
        in_specs=[vmem, smem, smem, smem, vmem, smem, vmem, vmem, vmem, vmem],
        out_specs=vmem,
        scratch_shapes=[
            pltpu.VMEM((2 * rows, nodes), BF16),
            pltpu.VMEM((parts * rows, W), BF16),
            pltpu.VMEM((parts * rows, W), BF16),
            pltpu.VMEM((W, (cells + 1) * W), BF16),
            pltpu.VMEM((W, 128), jnp.int32),
            pltpu.VMEM((cells + 8, W), jnp.int32),
            pltpu.VMEM((W, W), F32),
            pltpu.VMEM(((parts - 1) * rows, W), F32),
            pltpu.VMEM((2 * (parts - 1) * rows, UNROLL * W), BF16),
            pltpu.VMEM((cells * rows, W), BF16),
            pltpu.VMEM((cells * rows, W), F32),
            pltpu.VMEM((2, rows, W), BF16),
            pltpu.VMEM((2, rows, W), F32),
            pltpu.VMEM((2, rows, W), F32),
            pltpu.VMEM((rows, nodes), F32),
            pltpu.VMEM((n_mesh, rows, 2 * rows), F32),
            dma((2,)), dma((2,)), dma((2,)), dma((2,)), dma((2,)), dma((2,)),
            dma((n_mesh,)), dma((n_mesh,)),
        ],
        compiler_params=pltpu.CompilerParams(
            collective_id=0, has_side_effects=True, vmem_limit_bytes=48 * 1024 * 1024
        ),
    )(
        blocks, boundary_shift, centre, half_width, cell_matrix, cell_coef, connectivity,
        halo_list.reshape(1, -1), mass.reshape(1, -1), potential.reshape(1, -1),
    )


def solution(mesh):
    return jax.shard_map(
        body,
        mesh=mesh,
        in_specs=(
            P(("job", "cuts"), "mesh"),
            P(("job", "cuts")),
            P(("job", "cuts")),
            P(("job", "cuts")),
            P(),
            P(("job", "mesh")),
            P(None, ("job", "mesh")),
            P(("job", "mesh")),
            P(("job", "mesh")),
            P(("job", "mesh")),
        ),
        out_specs=P(("job", "cuts"), "mesh"),
        check_vma=False,
    )
```
